256 devices in a mesh: ctx: 32 (over y, x, z_hi), head: 8 (over z_lo, core).
Axes of the slice: x: 4, y: 4, z: 8 (z_hi: 2, z_lo: 4; z = z_hi * 4 + z_lo), core: 2. Of those that a mesh axis runs over, the one named last changes fastest.
Arguments:
- queries: bfloat16 [32768, 2048], P('ctx', 'head'), may hold values from -8 to 8
- keys: bfloat16 [32768, 2048], P('ctx', 'head'), may hold values from -8 to 8
- values: bfloat16 [32768, 2048], P('ctx', 'head'), may hold values from -6 to 6
- rates: float32 [32768, 8], P('ctx', 'head'), may hold values from 2 to 32
- doc_ids: int32 [32768], P('ctx'), may hold values from 0 to 15, never falling along the last dimension, each value on 1 to 4096 neighbouring positions
- windows: int32 [8], P('head'), may hold values from 256 to 1024, as said below
- fast_weights: float32 [3, 8, 256, 768], P(None, 'head', None, 'ctx'), may hold values from -0.375 to 0.375
- momentum: float32 [3, 8, 256, 768], P(None, 'head', None, 'ctx'), may hold values from -0.06 to 0.06
- out_gain: float32 [8, 256], P('head'), may hold values from 0.25 to 1.75
Outputs:
- mixed: bfloat16 [32768, 2048], P('ctx', 'head')
- new_weights: float32 [3, 8, 256, 768], P(None, 'head', None, 'ctx')
- new_momentum: float32 [3, 8, 256, 768], P(None, 'head', None, 'ctx')
The draws below stay inside these ranges and needn't reach their ends.
Inputs may be any that keep to these rules, and one draw needn't show every extreme that they name: `windows`: one head's window is exactly 1024.
All inputs are finite; a program needn't handle non-finite values.
Results may differ from the reference program's by a relative error of at most 0.022.
Values may be sent and summed in bfloat16 or wider, within the bound.
A program may use at most 64 MiB of HBM per device.

```python
import math
import jax
import jax.numpy as jnp
import numpy as np
from jax import lax

DH = 256
HID = 768
WIN = 1024
TOK_DEV = 1024
HEADS = 8
TOKENS = 32768


def draw_queries(key, part):
    key = jax.random.fold_in(key, 7)
    base = jnp.clip(jax.random.normal(key, (TOKENS, HEADS * DH), jnp.float32), -8.0, 8.0)
    return base.astype(jnp.bfloat16)


def draw_keys(key, part):
    key = jax.random.fold_in(key, 9)
    base = jnp.clip(jax.random.normal(key, (TOKENS, HEADS * DH), jnp.float32), -8.0, 8.0)
    return base.astype(jnp.bfloat16)


def draw_windows(key, part):
    key = jax.random.fold_in(key, 11)
    key_one, key_two = jax.random.split(key)
    spans = jax.random.randint(key_one, (HEADS,), WIN // 4, WIN + 1, dtype=jnp.int32)
    chosen = jax.random.randint(key_two, (), 0, HEADS, dtype=jnp.int32)
    return spans.at[chosen].set(WIN).astype(jnp.int32)


def level_of(key, extent, pieces, least, top_value):
    factor_of, own = 1.0, jax.random.fold_in(key, 6)
    for dim, blocks in pieces:
        heights = jnp.exp(jax.random.uniform(jax.random.fold_in(own, dim), (blocks,), jnp.float32, least / len(pieces), top_value / len(pieces)))
        factor_of = factor_of * jnp.repeat(heights, extent[dim] // blocks).reshape([-1 if axis == dim else 1 for axis in range(len(extent))])
    return factor_of


def split_up(amount, total, most, skew):
    weights = [(1 << 20) // math.isqrt(grade ** skew) + 1 for grade in range(2, amount + 1)]
    rest, given = total - most - (amount - 1), [1] * (amount - 1)
    while rest > 0:
        free = [i for i in range(amount - 1) if given[i] < most]
        whole, remaining = sum([weights[i] for i in free]), rest
        for i in free:
            addition = min(most - given[i], max(1, remaining * weights[i] // whole), rest)
            given[i] = given[i] + addition
            rest = rest - addition
    return np.array([most] + given)


def uneven_parts(rng, count, total, bound, skew):
    if count == 2:
        one = jax.random.randint(rng, (), max(1, total - bound), min(bound, total - 1) + 1)
        return jnp.stack([one, total - one])
    sizes = jnp.asarray(split_up(count, total, bound, skew), jnp.int32)
    twos = (count - 1) // 2
    giver, taker = sizes[1:1 + 2 * twos:2], sizes[2:2 + 2 * twos:2]
    slack = jnp.minimum(giver - 1, bound - taker)
    moved = jax.random.randint(jax.random.fold_in(rng, 1), (twos,), 0, 1 << 20) % (slack + 1)
    sizes = sizes.at[1:1 + 2 * twos:2].set(giver - moved).at[2:2 + 2 * twos:2].set(taker + moved)
    return sizes[jax.random.permutation(jax.random.fold_in(rng, 2), count)]


def normal_values(own_key, dims, deviation, most, cuts=(), held_as=jnp.bfloat16):
    values = deviation * jax.random.normal(own_key, dims, jnp.float32)
    if cuts:
        values = values * level_of(own_key, dims, cuts, -0.22, 0.18)
    return jnp.clip(values, -most, most).astype(held_as)


def setup_inputs(seed: int = 0) -> dict:
    streams_of = jax.random.split(jax.random.key(seed), 10)
    queries = draw_queries(jax.random.fold_in(streams_of[9], 71), 0)
    keys = draw_keys(jax.random.fold_in(streams_of[9], 71), 0)
    values = normal_values(streams_of[2], (TOKENS, HEADS * DH), 1.0, 6.0, ((0, 32), (1, 8)))
    rates = jnp.clip(jnp.exp(math.log(32.0) - 2.7725887 * jax.random.uniform(streams_of[3], (TOKENS, HEADS), jnp.float32) ** level_of(streams_of[3], (TOKENS, HEADS), ((0, 32), (1, 8)), -0.2, 0.2)), 2.0, 32.0)
    doc_ids = jnp.searchsorted(jnp.cumsum(uneven_parts(streams_of[4], max(2, TOKENS // (2 * TOK_DEV)), TOKENS, 4 * TOK_DEV, 2)), jnp.arange(TOKENS), side="right").astype(jnp.int32)
    windows = draw_windows(jax.random.fold_in(streams_of[9], 71), 0)
    fast_weights = normal_values(streams_of[6], (3, HEADS, DH, HID), DH ** -0.5, 0.375, ((1, 8), (3, 32)), jnp.float32)
    momentum = normal_values(streams_of[7], (3, HEADS, DH, HID), 0.01, 0.06, ((1, 8), (3, 32)), jnp.float32)
    out_gain = jnp.clip(1.0 + 0.15 * jax.random.normal(streams_of[8], (HEADS, DH), jnp.float32), 0.25, 1.75)
    return dict(queries=queries, keys=keys, values=values, rates=rates, doc_ids=doc_ids, windows=windows, fast_weights=fast_weights, momentum=momentum, out_gain=out_gain)


def silu_pair(gate_part):
    sigma = jax.nn.sigmoid(gate_part)
    return (gate_part * sigma, sigma * (1.0 + gate_part * (1.0 - sigma)))

def fast_update(key_rows, value_rows, rate_rows, old_bf, token_count):
    gate_part = jnp.dot(key_rows, old_bf[0], preferred_element_type=jnp.float32)
    up_part = jnp.dot(key_rows, old_bf[1], preferred_element_type=jnp.float32)
    active, slope = silu_pair(gate_part)
    hidden = (active * up_part).astype(jnp.bfloat16)
    d_pred = (-(rate_rows / token_count)[:, None] * value_rows.astype(jnp.float32)).astype(jnp.bfloat16)
    d_hidden = jnp.dot(d_pred, old_bf[2], preferred_element_type=jnp.float32)
    d_gate = (d_hidden * up_part * slope).astype(jnp.bfloat16)
    d_up = (d_hidden * active).astype(jnp.bfloat16)
    contract = (((0,), (0,)), ((), ()))
    return jnp.stack([lax.dot_general(key_rows, d_gate, contract, preferred_element_type=jnp.float32), lax.dot_general(key_rows, d_up, contract, preferred_element_type=jnp.float32), lax.dot_general(d_pred, hidden, contract, preferred_element_type=jnp.float32)])

def renorm(weights, moment, grad):
    new_moment = 0.9 * moment + grad
    stepped = weights - new_moment
    factor = jnp.sqrt(lax.optimization_barrier(jnp.mean(weights * weights, axis=-2, keepdims=True))) / jnp.sqrt(lax.optimization_barrier(jnp.mean(stepped * stepped, axis=-2, keepdims=True)) + 1e-06)
    return (stepped * factor, new_moment)

def fast_apply(query_rows, new_bf, gain_row):
    gate_part = jnp.dot(query_rows, new_bf[0], preferred_element_type=jnp.float32)
    up_part = jnp.dot(query_rows, new_bf[1], preferred_element_type=jnp.float32)
    hidden = (silu_pair(gate_part)[0] * up_part).astype(jnp.bfloat16)
    fast_out = lax.dot_general(hidden, new_bf[2], (((1,), (1,)), ((), ())), preferred_element_type=jnp.float32)
    return fast_out * lax.rsqrt(lax.optimization_barrier(jnp.mean(fast_out * fast_out, axis=-1, keepdims=True)) + 1e-06) * gain_row

def attend_block(query_block, key_block, value_block, query_docs, key_docs, query_pos, key_pos, window):
    scores = lax.dot_general(query_block, key_block, (((1,), (1,)), ((), ())), preferred_element_type=jnp.float32) * query_block.shape[1] ** (-0.5)
    allowed = (key_pos[None, :] >= 0) & (key_pos[None, :] <= query_pos[:, None])
    allowed = allowed & (key_pos[None, :] > query_pos[:, None] - window)
    allowed = allowed & (key_docs[None, :] == query_docs[:, None])
    scores = jnp.where(allowed, scores, -1e+30)
    top = lax.optimization_barrier(jnp.max(scores, axis=-1, keepdims=True))
    expo = jnp.where(allowed, jnp.exp(scores - top), 0.0)
    attn_weights = (expo / lax.optimization_barrier(jnp.sum(expo, axis=-1, keepdims=True))).astype(jnp.bfloat16)
    return jnp.dot(attn_weights, value_block, preferred_element_type=jnp.float32)

def by_head(array):
    return array.reshape(TOKENS, HEADS, DH).transpose(1, 0, 2)

def reference(queries, keys, values, rates, doc_ids, windows, fast_weights, momentum, out_gain):
    block_rows = min(512, TOK_DEV)
    num_blocks = TOKENS // block_rows

    def per_head(items):
        query_rows, key_rows, value_rows, rate_rows, weights, moment, gain_row, window = items
        grad = fast_update(key_rows, value_rows, rate_rows, weights.astype(jnp.bfloat16), TOKENS)
        new_w, new_m = renorm(weights, moment, grad)
        normed = fast_apply(query_rows, new_w.astype(jnp.bfloat16), gain_row)
        key_pad = jnp.pad(key_rows, ((WIN, 0), (0, 0)))
        value_pad = jnp.pad(value_rows, ((WIN, 0), (0, 0)))
        doc_pad = jnp.pad(doc_ids, (WIN, 0))

        def one_block(block_num):
            first = block_num * block_rows
            query_block = lax.dynamic_slice_in_dim(query_rows, first, block_rows, 0)
            key_block = lax.dynamic_slice_in_dim(key_pad, first, WIN + block_rows, 0)
            value_block = lax.dynamic_slice_in_dim(value_pad, first, WIN + block_rows, 0)
            key_docs = lax.dynamic_slice_in_dim(doc_pad, first, WIN + block_rows, 0)
            query_docs = lax.dynamic_slice_in_dim(doc_ids, first, block_rows, 0)
            query_pos = first + jnp.arange(block_rows, dtype=jnp.int32)
            key_pos = first - WIN + jnp.arange(WIN + block_rows, dtype=jnp.int32)
            return attend_block(query_block, key_block, value_block, query_docs, key_docs, query_pos, key_pos, window)
        attended = lax.map(one_block, jnp.arange(num_blocks, dtype=jnp.int32)).reshape(TOKENS, DH)
        return ((attended + normed).astype(jnp.bfloat16), new_w, new_m)
    mixed, new_w, new_m = lax.map(per_head, (by_head(queries), by_head(keys), by_head(values), rates.T, fast_weights.transpose(1, 0, 2, 3), momentum.transpose(1, 0, 2, 3), out_gain, windows))
    mixed = mixed.transpose(1, 0, 2).reshape(TOKENS, HEADS * DH)
    return (mixed, new_w.transpose(1, 0, 2, 3), new_m.transpose(1, 0, 2, 3))
```

```python
import functools
import math

import jax
import jax.numpy as jnp
from jax import lax
from jax.experimental import pallas as pl
from jax.experimental.pallas import tpu as pltpu
from jax.sharding import PartitionSpec as P

DH = 256
HID = 768
TOK = 1024
SHARE = 24
PAIR = 48
TOKENS = 32768
BLK = 256
NBLK = TOK // BLK
MESH = pl.DeviceIdType.MESH
SCALE = math.log2(math.e) / 16.0
NEG = -1e30
F32 = jnp.float32
BF16 = jnp.bfloat16

ZW, ZM, ZG, HDOC = 0, 1, 2, 3
HK, HV = 4, 8
AG1, RS, AG2 = 12, 24, 36
NSEM = 48


def dot_nn(a, b):
    return jnp.dot(a, b, preferred_element_type=F32)


def dot_nt(a, b):
    return lax.dot_general(a, b, (((1,), (1,)), ((), ())), preferred_element_type=F32)


def kernel(
    win_ref, q_ref, k_ref, v_ref, rate_ref, doc_ref, w_ref, m_ref, gain_ref,
    out_ref, nw_ref, nm_ref,
    kt, dp, dpt, kh, vh, doch, dcol,
    wz, mz, wzr, mzr, wp, mp,
    wall, wnew, grad, rs1, rs2s, rs2, tot, totb, totz, nwp, nmp,
    acc, m_s, l_s, normed,
    ssem, rsem,
):
    c, h = lax.axis_index("ctx"), lax.axis_index("head")
    y, x, zh = c // 8, (c // 2) % 4, c % 2
    zpeer = c + 1 - 2 * zh
    nxt, prv = (c + 1) % 32, (c + 31) % 32
    other = (c + 31 + 2 * zh) % 32
    xpeer = [y * 8 + ((x + d) % 4) * 2 + zh for d in (1, 2, 3)]
    ypeer = [((y + d) % 4) * 8 + x * 2 + zh for d in (1, 2, 3)]

    barrier = pltpu.get_barrier_semaphore()
    for peer in [zpeer, other] + xpeer + ypeer:
        pl.semaphore_signal(barrier, inc=1, device_id=(peer, h), device_id_type=MESH)

    def rcopy(src, dst, num, ctx):
        return pltpu.make_async_remote_copy(
            src_ref=src, dst_ref=dst, send_sem=ssem.at[num], recv_sem=rsem.at[num],
            device_id=(ctx, h), device_id_type=MESH,
        )

    started = []

    def start(src, dst, num, ctx):
        copy = rcopy(src, dst, num, ctx)
        copy.start()
        started.append(copy)
        return copy

    own = pl.ds(pl.multiple_of(zh * SHARE, 8), SHARE)
    far = pl.ds(pl.multiple_of((1 - zh) * SHARE, 8), SHARE)
    pad = jnp.zeros((8, DH), F32)
    shares = []
    for ref, full, sent in ((w_ref, wp, wz), (m_ref, mp, mz)):
        rows = [ref[j].T for j in range(3)]
        for j in range(3):
            full[j, own, :] = rows[j]
        sent[...] = jnp.concatenate(rows + [pad], axis=0).astype(BF16)

    pl.semaphore_wait(barrier, 8)
    cw = start(wz, wzr, ZW, zpeer)
    cm = start(mz, mzr, ZM, zpeer)
    hdoc = start(doc_ref, doch, HDOC, nxt)
    halo = {}
    for b in reversed(range(NBLK)):
        rows = pl.ds(b * BLK, BLK)
        halo[b] = (
            start(k_ref.at[rows], kh.at[rows], HK + b, nxt),
            start(v_ref.at[rows], vh.at[rows], HV + b, nxt),
        )

    def gather_first(buf, base):
        return [
            start(buf.at[0, :, y, x], buf.at[0, :, y, x], base + d, xpeer[d]) for d in range(3)
        ] + [
            start(buf.at[1, :, y, x], buf.at[1, :, y, x], base + 3 + d, ypeer[d]) for d in range(3)
        ]

    def gather_second(buf, base, first):
        for copy in first[:3]:
            copy.wait_recv()
        copies = [
            start(buf.at[0, :, y], buf.at[0, :, y], base + 6 + d, ypeer[d]) for d in range(3)
        ]
        for copy in first[3:]:
            copy.wait_recv()
        copies += [
            start(buf.at[1, :, :, x], buf.at[1, :, :, x], base + 9 + d, xpeer[d])
            for d in range(3)
        ]
        return copies

    def set_pair(buf, value):
        value = value.astype(BF16)
        buf[0, :, y, x] = value[:, :, :128]
        buf[1, :, y, x] = value[:, :, 128:]

    def matrix(buf, j):
        return jnp.concatenate(
            [buf[0, j].reshape(HID, 128), buf[1, j].reshape(HID, 128)], axis=-1
        )

    kt[...] = k_ref[...].T
    pred = (-(rate_ref[...] / TOKENS) * v_ref[...].astype(F32)).astype(BF16)
    dp[...] = pred
    dpt[...] = pred.T
    dcol[...] = jnp.broadcast_to(doc_ref[...].astype(F32), (128, TOK)).T

    cw.wait_recv()
    got = wzr[...].astype(F32)
    for j in range(3):
        wp[j, far, :] = got[j * SHARE : (j + 1) * SHARE]
    set_pair(wall, wp[...])
    first = gather_first(wall, AG1)

    window = win_ref[0]

    def attend_own(b):
        n = (b + 1) * BLK
        rows = pl.ds(b * BLK, BLK)
        scores = dot_nn(q_ref[rows, :], kt[:, :n])
        qpos = b * BLK + lax.broadcasted_iota(jnp.int32, (BLK, 1), 0)
        kpos = lax.broadcasted_iota(jnp.int32, (1, n), 1)
        allowed = (kpos <= qpos) & (kpos > qpos - window)
        allowed = allowed & (doc_ref[:, :n].astype(F32) == dcol[rows, 0:1])
        scores = jnp.where(allowed, scores, NEG)
        top = jnp.max(scores, axis=-1, keepdims=True)
        expo = jnp.exp2((scores - top) * SCALE)
        m_s[rows, :] = top
        l_s[rows, :] = jnp.sum(expo, axis=-1, keepdims=True)
        acc[rows, :] = dot_nn(expo.astype(BF16), v_ref[:n, :])

    def attend_halo(b):
        for copy in halo[b]:
            copy.wait_recv()
        krows = pl.ds(b * BLK, BLK)
        keys, values = kh[krows, :], vh[krows, :]
        kdoc = doch[:, b * BLK : (b + 1) * BLK].astype(F32)
        reach = jnp.where(c == 0, -4 * TOK, window)

        def body(i, carry):
            rows = pl.ds(pl.multiple_of(i * BLK, BLK), BLK)
            scores = dot_nt(q_ref[rows, :], keys)
            qpos = i * BLK + lax.broadcasted_iota(jnp.int32, (BLK, 1), 0)
            kpos = b * BLK - TOK + lax.broadcasted_iota(jnp.int32, (1, BLK), 1)
            allowed = (kpos > qpos - reach) & (kdoc == dcol[rows, 0:1])
            scores = jnp.where(allowed, scores, NEG)
            old = m_s[rows, :]
            top = jnp.maximum(old, jnp.max(scores, axis=-1, keepdims=True))
            expo = jnp.exp2((scores - top) * SCALE)
            alpha = jnp.exp2((old - top) * SCALE)
            m_s[rows, :] = top
            l_s[rows, :] = l_s[rows, :] * alpha + jnp.sum(expo, axis=-1, keepdims=True)
            acc[rows, :] = acc[rows, :] * alpha + dot_nn(expo.astype(BF16), values)
            return carry

        lax.fori_loop(0, b + 1, body, 0)

    attend_own(0)
    attend_own(1)
    second = gather_second(wall, AG1, first)
    attend_own(2)
    attend_own(3)
    cm.wait_recv()
    got = mzr[...].astype(F32)
    for j in range(3):
        mp[j, far, :] = got[j * SHARE : (j + 1) * SHARE]
    for copy in second:
        copy.wait_recv()

    def update(yy, carry):
        def part(j):
            return jnp.concatenate(
                [wall[0, j, yy].reshape(192, 128), wall[1, j, yy].reshape(192, 128)], axis=-1
            )

        gate = dot_nn(part(0), kt[...])
        up = dot_nn(part(1), kt[...])
        back = dot_nn(part(2), dpt[...])
        sig = 0.5 * jnp.tanh(0.5 * gate) + 0.5
        active = gate * sig
        hidden = (active * up).astype(BF16)
        d_gate = (back * up * (sig + active * (1.0 - sig))).astype(BF16)
        d_up = (back * active).astype(BF16)
        for j, g in enumerate(
            (dot_nn(d_gate, k_ref[...]), dot_nn(d_up, k_ref[...]), dot_nn(hidden, dp[...]))
        ):
            g = g.astype(BF16).reshape(4, PAIR, DH)
            grad[0, j, yy] = g[:, :, :128]
            grad[1, j, yy] = g[:, :, 128:]
        return carry

    lax.fori_loop(0, 4, update, 0)

    r1a = [
        start(grad.at[0, :, (y + d + 1) % 4], rs1.at[0, d], RS + d, ypeer[d]) for d in range(3)
    ]
    r1b = [
        start(grad.at[1, :, :, (x + d + 1) % 4], rs1.at[1, d], RS + 3 + d, xpeer[d])
        for d in range(3)
    ]
    for copy in r1a:
        copy.wait_recv()
    rs2s[0] = sum([rs1[0, d].astype(F32) for d in range(3)], grad[0, :, y].astype(F32)).astype(
        BF16
    )
    r2a = [
        start(rs2s.at[0, :, (x + d + 1) % 4], rs2.at[0, d], RS + 6 + d, xpeer[d]) for d in range(3)
    ]
    for copy in r1b:
        copy.wait_recv()
    rs2s[1] = sum(
        [rs1[1, d].astype(F32) for d in range(3)], grad[1, :, :, x].astype(F32)
    ).astype(BF16)
    r2b = [
        start(rs2s.at[1, :, (y + d + 1) % 4], rs2.at[1, d], RS + 9 + d, ypeer[d]) for d in range(3)
    ]
    for copy in r2a:
        copy.wait_recv()
    tot[:, :, :128] = sum([rs2[0, d].astype(F32) for d in range(3)], rs2s[0, :, x].astype(F32))
    for copy in r2b:
        copy.wait_recv()
    tot[:, :, 128:] = sum([rs2[1, d].astype(F32) for d in range(3)], rs2s[1, :, y].astype(F32))
    totb[...] = tot[...].astype(BF16)
    cz = start(totb, totz, ZG, zpeer)
    hdoc.wait_recv()
    cz.wait_recv()

    weights = wp[...]
    moment = 0.9 * mp[...] + (tot[...] + totz[...].astype(F32))
    stepped = weights - moment
    factor = jnp.sqrt(jnp.mean(weights * weights, axis=-1, keepdims=True)) / jnp.sqrt(
        jnp.mean(stepped * stepped, axis=-1, keepdims=True) + 1e-06
    )
    fresh = stepped * factor
    set_pair(wnew, fresh)
    first = gather_first(wnew, AG2)
    nwp[...] = fresh
    nmp[...] = moment
    for j in range(3):
        nw_ref[j] = nwp[j, own, :].T
        nm_ref[j] = nmp[j, own, :].T
    second = gather_second(wnew, AG2, first)
    attend_halo(3)
    for copy in second:
        copy.wait_recv()

    new_gate, new_up, new_down = matrix(wnew, 0), matrix(wnew, 1), matrix(wnew, 2)
    gain = gain_ref[...]
    for b in range(NBLK):
        rows = pl.ds(b * BLK, BLK)
        gate = dot_nt(q_ref[rows, :], new_gate)
        up = dot_nt(q_ref[rows, :], new_up)
        sig = 0.5 * jnp.tanh(0.5 * gate) + 0.5
        fast = dot_nn((gate * sig * up).astype(BF16), new_down)
        mean = jnp.mean(fast * fast, axis=-1, keepdims=True)
        normed[rows, :] = fast * lax.rsqrt(mean + 1e-06) * gain

    for b in (2, 1, 0):
        attend_halo(b)
    for b in range(NBLK):
        rows = pl.ds(b * BLK, BLK)
        out_ref[rows, :] = (acc[rows, :] / l_s[rows, :] + normed[rows, :]).astype(BF16)
    for copy in started:
        copy.wait_send()


def local(queries, keys, values, rates, doc_ids, windows, fast_weights, momentum, out_gain):
    vmem = pl.BlockSpec(memory_space=pltpu.VMEM)
    smem = pl.BlockSpec(memory_space=pltpu.SMEM)
    plane = (2, 3, 4, 4, PAIR, 128)
    mixed, new_w, new_m = pl.pallas_call(
        kernel,
        out_shape=(
            jax.ShapeDtypeStruct((TOK, DH), BF16),
            jax.ShapeDtypeStruct((3, DH, SHARE), F32),
            jax.ShapeDtypeStruct((3, DH, SHARE), F32),
        ),
        in_specs=[smem] + [vmem] * 8,
        out_specs=(vmem, vmem, vmem),
        scratch_shapes=[
            pltpu.VMEM((DH, TOK), BF16),
            pltpu.VMEM((TOK, DH), BF16),
            pltpu.VMEM((DH, TOK), BF16),
            pltpu.VMEM((TOK, DH), BF16),
            pltpu.VMEM((TOK, DH), BF16),
            pltpu.VMEM((1, TOK), jnp.int32),
            pltpu.VMEM((TOK, 128), F32),
            pltpu.VMEM((80, DH), BF16),
            pltpu.VMEM((80, DH), BF16),
            pltpu.VMEM((80, DH), BF16),
            pltpu.VMEM((80, DH), BF16),
            pltpu.VMEM((3, PAIR, DH), F32),
            pltpu.VMEM((3, PAIR, DH), F32),
            pltpu.VMEM(plane, BF16),
            pltpu.VMEM(plane, BF16),
            pltpu.VMEM(plane, BF16),
            pltpu.VMEM((2, 3, 3, 4, PAIR, 128), BF16),
            pltpu.VMEM((2, 3, 4, PAIR, 128), BF16),
            pltpu.VMEM((2, 3, 3, PAIR, 128), BF16),
            pltpu.VMEM((3, PAIR, DH), F32),
            pltpu.VMEM((3, PAIR, DH), BF16),
            pltpu.VMEM((3, PAIR, DH), BF16),
            pltpu.VMEM((3, PAIR, DH), F32),
            pltpu.VMEM((3, PAIR, DH), F32),
            pltpu.VMEM((TOK, DH), F32),
            pltpu.VMEM((TOK, 1), F32),
            pltpu.VMEM((TOK, 1), F32),
            pltpu.VMEM((TOK, DH), F32),
            pltpu.SemaphoreType.DMA((NSEM,)),
            pltpu.SemaphoreType.DMA((NSEM,)),
        ],
        compiler_params=pltpu.CompilerParams(
            collective_id=0, has_side_effects=True, vmem_limit_bytes=56 * 2**20
        ),
        name="ttt_layer",
    )(
        windows,
        queries,
        keys,
        values,
        rates,
        doc_ids.reshape(1, TOK),
        fast_weights.reshape(3, DH, SHARE),
        momentum.reshape(3, DH, SHARE),
        out_gain,
    )
    return mixed, new_w.reshape(3, 1, DH, SHARE), new_m.reshape(3, 1, DH, SHARE)


def solution(mesh):
    in_specs = (
        P("ctx", "head"),
        P("ctx", "head"),
        P("ctx", "head"),
        P("ctx", "head"),
        P("ctx"),
        P("head"),
        P(None, "head", None, "ctx"),
        P(None, "head", None, "ctx"),
        P("head", None),
    )
    out_specs = (P("ctx", "head"), P(None, "head", None, "ctx"), P(None, "head", None, "ctx"))
    return jax.shard_map(local, mesh=mesh, in_specs=in_specs, out_specs=out_specs, check_vma=False)
```

```python
import functools
import math

import jax
import jax.numpy as jnp
from jax import lax
from jax.experimental import pallas as pl
from jax.experimental.pallas import tpu as pltpu
from jax.sharding import PartitionSpec as P

DH = 256
HID = 768
TOK = 1024
SHARE = 24
PAIR = 48
TOKENS = 32768
BLK = 256
NBLK = TOK // BLK
MESH = pl.DeviceIdType.MESH
SCALE = math.log2(math.e) / 16.0
NEG = -1e30
SENDS = ((0, 4), (4, 6), (6, 8))
F32 = jnp.float32
BF16 = jnp.bfloat16

ZW, ZM, HDOC, ZG = 0, 1, 2, 3
HK, HV = 5, 9
AG1, RS, AG2 = 13, 25, 37
NSEM = 49


def dot_nn(a, b):
    return jnp.dot(a, b, preferred_element_type=F32)


def dot_nt(a, b):
    return lax.dot_general(a, b, (((1,), (1,)), ((), ())), preferred_element_type=F32)


def kernel(
    win_ref, q_ref, k_ref, v_ref, rate_ref, doc_ref, w_ref, m_ref, gain_ref,
    out_ref, nw_ref, nm_ref,
    kt, dp, dpt, kh, vh, doch, dcol,
    wz, mz, wzr, mzr, wp, mp,
    wall, wnew, grad, rs1, rs2s, rs2, tot, totb, totz, nwp, nmp,
    acc, m_s, l_s, normed,
    ssem, rsem,
):
    c, h = lax.axis_index("ctx"), lax.axis_index("head")
    y, x, zh = c // 8, (c // 2) % 4, c % 2
    zpeer = c + 1 - 2 * zh
    nxt, prv = (c + 1) % 32, (c + 31) % 32
    other = (c + 31 + 2 * zh) % 32
    xpeer = [y * 8 + ((x + d) % 4) * 2 + zh for d in (1, 2, 3)]
    ypeer = [((y + d) % 4) * 8 + x * 2 + zh for d in (1, 2, 3)]

    barrier = pltpu.get_barrier_semaphore()
    for peer in [zpeer, other] + xpeer + ypeer:
        pl.semaphore_signal(barrier, inc=1, device_id=(peer, h), device_id_type=MESH)

    def rcopy(src, dst, num, ctx):
        return pltpu.make_async_remote_copy(
            src_ref=src, dst_ref=dst, send_sem=ssem.at[num], recv_sem=rsem.at[num],
            device_id=(ctx, h), device_id_type=MESH,
        )

    started = []

    def start(src, dst, num, ctx):
        copy = rcopy(src, dst, num, ctx)
        copy.start()
        started.append(copy)
        return copy

    own = pl.ds(pl.multiple_of(zh * SHARE, 8), SHARE)
    far = pl.ds(pl.multiple_of((1 - zh) * SHARE, 8), SHARE)
    pad = jnp.zeros((8, DH), F32)
    shares = []
    for ref, full, sent in ((w_ref, wp, wz), (m_ref, mp, mz)):
        rows = [ref[j] for j in range(3)]
        for j in range(3):
            full[j, own, :] = rows[j]
        sent[...] = jnp.concatenate(rows + [pad], axis=0).astype(BF16)

    pl.semaphore_wait(barrier, 8)
    cw = start(wz, wzr, ZW, zpeer)
    cm = start(mz, mzr, ZM, zpeer)
    hdoc = start(doc_ref, doch, HDOC, nxt)
    order = [(b, kv) for b in reversed(range(NBLK)) for kv in (0, 1)]
    halo = {b: [] for b in range(NBLK)}

    def send_halo(first, last):
        for b, kv in order[first:last]:
            rows = pl.ds(b * BLK, BLK)
            src, dst, num = ((k_ref, kh, HK), (v_ref, vh, HV))[kv]
            halo[b].append(start(src.at[rows], dst.at[rows], num + b, nxt))

    def gather_first(buf, base):
        return [
            start(buf.at[0, :, y, x], buf.at[0, :, y, x], base + d, xpeer[d]) for d in range(3)
        ] + [
            start(buf.at[1, :, y, x], buf.at[1, :, y, x], base + 3 + d, ypeer[d]) for d in range(3)
        ]

    def gather_second(buf, base, first):
        for copy in first[:3]:
            copy.wait_recv()
        copies = [
            start(buf.at[0, :, y], buf.at[0, :, y], base + 6 + d, ypeer[d]) for d in range(3)
        ]
        for copy in first[3:]:
            copy.wait_recv()
        copies += [
            start(buf.at[1, :, :, x], buf.at[1, :, :, x], base + 9 + d, xpeer[d])
            for d in range(3)
        ]
        return copies

    def set_pair(buf, value):
        value = value.astype(BF16)
        buf[0, :, y, x] = value[:, :, :128]
        buf[1, :, y, x] = value[:, :, 128:]

    def matrix(buf, j):
        return jnp.concatenate(
            [buf[0, j].reshape(HID, 128), buf[1, j].reshape(HID, 128)], axis=-1
        )

    kt[...] = k_ref[...].T
    pred = (-(rate_ref[...] / TOKENS) * v_ref[...].T.astype(F32)).astype(BF16)
    dpt[...] = pred
    dp[...] = pred.T
    dcol[...] = jnp.broadcast_to(doc_ref[...].astype(F32), (128, TOK)).T

    window = win_ref[0]

    def attend_own(b):
        n = (b + 1) * BLK
        rows = pl.ds(b * BLK, BLK)
        scores = dot_nn(q_ref[rows, :], kt[:, :n])
        qpos = b * BLK + lax.broadcasted_iota(jnp.int32, (BLK, 1), 0)
        kpos = lax.broadcasted_iota(jnp.int32, (1, n), 1)
        allowed = (kpos <= qpos) & (kpos > qpos - window)
        allowed = allowed & (doc_ref[:, :n].astype(F32) == dcol[rows, 0:1])
        scores = jnp.where(allowed, scores, NEG)
        top = jnp.max(scores, axis=-1, keepdims=True)
        expo = jnp.exp2((scores - top) * SCALE)
        m_s[rows, :] = top
        l_s[rows, :] = jnp.sum(expo, axis=-1, keepdims=True)
        acc[rows, :] = dot_nn(expo.astype(BF16), v_ref[:n, :])

    def attend_halo(b):
        for copy in halo[b]:
            copy.wait_recv()
        krows = pl.ds(b * BLK, BLK)
        keys, values = kh[krows, :], vh[krows, :]
        kdoc = doch[:, b * BLK : (b + 1) * BLK].astype(F32)
        reach = jnp.where(c == 0, -4 * TOK, window)

        def body(i, carry):
            rows = pl.ds(pl.multiple_of(i * BLK, BLK), BLK)
            scores = dot_nt(q_ref[rows, :], keys)
            qpos = i * BLK + lax.broadcasted_iota(jnp.int32, (BLK, 1), 0)
            kpos = b * BLK - TOK + lax.broadcasted_iota(jnp.int32, (1, BLK), 1)
            allowed = (kpos > qpos - reach) & (kdoc == dcol[rows, 0:1])
            scores = jnp.where(allowed, scores, NEG)
            old = m_s[rows, :]
            top = jnp.maximum(old, jnp.max(scores, axis=-1, keepdims=True))
            expo = jnp.exp2((scores - top) * SCALE)
            alpha = jnp.exp2((old - top) * SCALE)
            m_s[rows, :] = top
            l_s[rows, :] = l_s[rows, :] * alpha + jnp.sum(expo, axis=-1, keepdims=True)
            acc[rows, :] = acc[rows, :] * alpha + dot_nn(expo.astype(BF16), values)
            return carry

        lax.fori_loop(0, b + 1, body, 0)

    attend_own(0)
    attend_own(1)
    cw.wait_recv()
    got = wzr[...].astype(F32)
    for j in range(3):
        wp[j, far, :] = got[j * SHARE : (j + 1) * SHARE]
    set_pair(wall, wp[...])
    first = gather_first(wall, AG1)
    send_halo(*SENDS[0])
    attend_own(2)
    second = gather_second(wall, AG1, first)
    attend_own(3)
    cm.wait_recv()
    got = mzr[...].astype(F32)
    for j in range(3):
        mp[j, far, :] = got[j * SHARE : (j + 1) * SHARE]
    for copy in second:
        copy.wait_recv()

    def update(d, carry):
        yy = (y + 1 + d) % 4

        def part(j):
            return jnp.concatenate(
                [wall[0, j, yy].reshape(192, 128), wall[1, j, yy].reshape(192, 128)], axis=-1
            )

        gate = dot_nn(part(0), kt[...])
        up = dot_nn(part(1), kt[...])
        back = dot_nn(part(2), dpt[...])
        sig = 0.5 * jnp.tanh(0.5 * gate) + 0.5
        active = gate * sig
        hidden = (active * up).astype(BF16)
        d_gate = (back * up * (sig + active * (1.0 - sig))).astype(BF16)
        d_up = (back * active).astype(BF16)
        for j, g in enumerate(
            (dot_nn(d_gate, k_ref[...]), dot_nn(d_up, k_ref[...]), dot_nn(hidden, dp[...]))
        ):
            g = g.astype(BF16).reshape(4, PAIR, DH)
            grad[0, j, yy] = g[:, :, :128]
            grad[1, j, yy] = g[:, :, 128:]

        @pl.when(d < 3)
        def _():
            rcopy(grad.at[0, :, yy], rs1.at[0, d], RS + d, yy * 8 + x * 2 + zh).start()

        for e in range(3):
            rcopy(
                grad.at[1, :, yy, (x + e + 1) % 4], rs1.at[1, e, :, yy], RS + 3 + e, xpeer[e]
            ).start()
        return carry

    lax.fori_loop(0, 4, update, 0)

    r1a = [
        rcopy(grad.at[0, :, (y + d + 1) % 4], rs1.at[0, d], RS + d, ypeer[d]) for d in range(3)
    ]
    r1b = [
        rcopy(grad.at[1, :, :, (x + d + 1) % 4], rs1.at[1, d], RS + 3 + d, xpeer[d])
        for d in range(3)
    ]
    started.extend(r1a + r1b)
    send_halo(*SENDS[1])
    for copy in r1a:
        copy.wait_recv()
    rs2s[0] = sum([rs1[0, d].astype(F32) for d in range(3)], grad[0, :, y].astype(F32)).astype(
        BF16
    )
    r2a = [
        start(rs2s.at[0, :, (x + d + 1) % 4], rs2.at[0, d], RS + 6 + d, xpeer[d]) for d in range(3)
    ]
    for copy in r1b:
        copy.wait_recv()
    rs2s[1] = sum(
        [rs1[1, d].astype(F32) for d in range(3)], grad[1, :, :, x].astype(F32)
    ).astype(BF16)
    r2b = [
        start(rs2s.at[1, :, (y + d + 1) % 4], rs2.at[1, d], RS + 9 + d, ypeer[d]) for d in range(3)
    ]
    cz = []
    for half, copies, mine in ((0, r2a, x), (1, r2b, y)):
        lanes = slice(half * 128, half * 128 + 128)
        for copy in copies:
            copy.wait_recv()
        value = sum([rs2[half, d].astype(F32) for d in range(3)], rs2s[half, :, mine].astype(F32))
        tot[:, :, lanes] = value
        totb[half] = value.astype(BF16)
        cz.append(start(totb.at[half], totz.at[half], ZG + half, zpeer))
    send_halo(*SENDS[2])
    hdoc.wait_recv()
    attend_halo(3)
    for copy in cz:
        copy.wait_recv()
    tot[...] += jnp.concatenate([totz[0], totz[1]], axis=-1).astype(F32)

    weights = wp[...]
    moment = 0.9 * mp[...] + tot[...]
    stepped = weights - moment
    factor = jnp.sqrt(jnp.mean(weights * weights, axis=-1, keepdims=True)) / jnp.sqrt(
        jnp.mean(stepped * stepped, axis=-1, keepdims=True) + 1e-06
    )
    fresh = stepped * factor
    set_pair(wnew, fresh)
    first = gather_first(wnew, AG2)
    nwp[...] = fresh
    nmp[...] = moment
    for j in range(3):
        nw_ref[j] = nwp[j, own, :]
        nm_ref[j] = nmp[j, own, :]
    second = gather_second(wnew, AG2, first)
    attend_halo(2)
    for copy in second:
        copy.wait_recv()

    new_gate, new_up, new_down = matrix(wnew, 0), matrix(wnew, 1), matrix(wnew, 2)
    gain = gain_ref[...]
    for b in range(NBLK):
        rows = pl.ds(b * BLK, BLK)
        gate = dot_nt(q_ref[rows, :], new_gate)
        up = dot_nt(q_ref[rows, :], new_up)
        sig = 0.5 * jnp.tanh(0.5 * gate) + 0.5
        fast = dot_nn((gate * sig * up).astype(BF16), new_down)
        mean = jnp.mean(fast * fast, axis=-1, keepdims=True)
        normed[rows, :] = fast * lax.rsqrt(mean + 1e-06) * gain

    for b in (1, 0):
        attend_halo(b)
    for b in range(NBLK):
        rows = pl.ds(b * BLK, BLK)
        out_ref[rows, :] = (acc[rows, :] / l_s[rows, :] + normed[rows, :]).astype(BF16)
    for copy in started:
        copy.wait_send()


def local(queries, keys, values, rates, doc_ids, windows, fast_weights, momentum, out_gain):
    vmem = pl.BlockSpec(memory_space=pltpu.VMEM)
    smem = pl.BlockSpec(memory_space=pltpu.SMEM)
    plane = (2, 3, 4, 4, PAIR, 128)
    mixed, new_w, new_m = pl.pallas_call(
        kernel,
        out_shape=(
            pltpu.VMEM((TOK, DH), BF16),
            pltpu.VMEM((3, SHARE, DH), F32),
            pltpu.VMEM((3, SHARE, DH), F32),
        ),
        in_specs=[smem] + [vmem] * 8,
        out_specs=(vmem, vmem, vmem),
        scratch_shapes=[
            pltpu.VMEM((DH, TOK), BF16),
            pltpu.VMEM((TOK, DH), BF16),
            pltpu.VMEM((DH, TOK), BF16),
            pltpu.VMEM((TOK, DH), BF16),
            pltpu.VMEM((TOK, DH), BF16),
            pltpu.VMEM((1, TOK), jnp.int32),
            pltpu.VMEM((TOK, 128), F32),
            pltpu.VMEM((80, DH), BF16),
            pltpu.VMEM((80, DH), BF16),
            pltpu.VMEM((80, DH), BF16),
            pltpu.VMEM((80, DH), BF16),
            pltpu.VMEM((3, PAIR, DH), F32),
            pltpu.VMEM((3, PAIR, DH), F32),
            pltpu.VMEM(plane, BF16),
            pltpu.VMEM(plane, BF16),
            pltpu.VMEM(plane, BF16),
            pltpu.VMEM((2, 3, 3, 4, PAIR, 128), BF16),
            pltpu.VMEM((2, 3, 4, PAIR, 128), BF16),
            pltpu.VMEM((2, 3, 3, PAIR, 128), BF16),
            pltpu.VMEM((3, PAIR, DH), F32),
            pltpu.VMEM((2, 3, PAIR, 128), BF16),
            pltpu.VMEM((2, 3, PAIR, 128), BF16),
            pltpu.VMEM((3, PAIR, DH), F32),
            pltpu.VMEM((3, PAIR, DH), F32),
            pltpu.VMEM((TOK, DH), F32),
            pltpu.VMEM((TOK, 1), F32),
            pltpu.VMEM((TOK, 1), F32),
            pltpu.VMEM((TOK, DH), F32),
            pltpu.SemaphoreType.DMA((NSEM,)),
            pltpu.SemaphoreType.DMA((NSEM,)),
        ],
        compiler_params=pltpu.CompilerParams(
            collective_id=0, has_side_effects=True, vmem_limit_bytes=56 * 2**20
        ),
        name="ttt_layer",
    )(
        windows,
        queries,
        keys,
        values,
        rates.reshape(1, TOK),
        doc_ids.reshape(1, TOK),
        fast_weights.reshape(3, DH, SHARE).transpose(0, 2, 1),
        momentum.reshape(3, DH, SHARE).transpose(0, 2, 1),
        out_gain,
    )
    new_w, new_m = (
        part.transpose(0, 2, 1).reshape(3, 1, DH, SHARE) for part in (new_w, new_m)
    )
    return mixed, new_w, new_m


def solution(mesh):
    in_specs = (
        P("ctx", "head"),
        P("ctx", "head"),
        P("ctx", "head"),
        P("ctx", "head"),
        P("ctx"),
        P("head"),
        P(None, "head", None, "ctx"),
        P(None, "head", None, "ctx"),
        P("head", None),
    )
    out_specs = (P("ctx", "head"), P(None, "head", None, "ctx"), P(None, "head", None, "ctx"))
    return jax.shard_map(local, mesh=mesh, in_specs=in_specs, out_specs=out_specs, check_vma=False)
```

```python
import functools
import math

import jax
import jax.numpy as jnp
from jax import lax
from jax.experimental import pallas as pl
from jax.experimental.pallas import tpu as pltpu
from jax.sharding import PartitionSpec as P

DH = 256
HID = 768
TOK = 1024
SHARE = 24
PAIR = 48
TOKENS = 32768
BLK = 256
NBLK = TOK // BLK
MESH = pl.DeviceIdType.MESH
SCALE = math.log2(math.e) / 16.0
NEG = -1e30
SENDS = ((0, 6), (6, 6), (6, 8))
F32 = jnp.float32
BF16 = jnp.bfloat16

ZW, ZM, HDOC, ZG = 0, 1, 2, 3
HK, HV = 5, 9
AG1, RS, AG2 = 13, 25, 37
NSEM = 49


def dot_nn(a, b):
    return jnp.dot(a, b, preferred_element_type=F32)


def dot_nt(a, b):
    return lax.dot_general(a, b, (((1,), (1,)), ((), ())), preferred_element_type=F32)


def kernel(
    win_ref, q_ref, k_ref, v_ref, rate_ref, doc_ref, w_ref, m_ref, gain_ref,
    out_ref, nw_ref, nm_ref,
    kt, dp, dpt, kh, vh, doch, dcol,
    wz, mz, wzr, mzr, wp, mp,
    wall, wnew, grad, rs1, rs2s, rs2, tot, totb, totz, nwp, nmp,
    acc, m_s, l_s, normed,
    ssem, rsem,
):
    c, h = lax.axis_index("ctx"), lax.axis_index("head")
    y, x, zh = c // 8, (c // 2) % 4, c % 2
    zpeer = c + 1 - 2 * zh
    nxt, prv = (c + 1) % 32, (c + 31) % 32
    other = (c + 31 + 2 * zh) % 32
    xpeer = [y * 8 + ((x + d) % 4) * 2 + zh for d in (1, 2, 3)]
    ypeer = [((y + d) % 4) * 8 + x * 2 + zh for d in (1, 2, 3)]

    barrier = pltpu.get_barrier_semaphore()
    for peer in [zpeer, other] + xpeer + ypeer:
        pl.semaphore_signal(barrier, inc=1, device_id=(peer, h), device_id_type=MESH)

    def rcopy(src, dst, num, ctx):
        return pltpu.make_async_remote_copy(
            src_ref=src, dst_ref=dst, send_sem=ssem.at[num], recv_sem=rsem.at[num],
            device_id=(ctx, h), device_id_type=MESH,
        )

    started = []

    def start(src, dst, num, ctx):
        copy = rcopy(src, dst, num, ctx)
        copy.start()
        started.append(copy)
        return copy

    own = pl.ds(pl.multiple_of(zh * SHARE, 8), SHARE)
    far = pl.ds(pl.multiple_of((1 - zh) * SHARE, 8), SHARE)
    pad = jnp.zeros((8, DH), F32)
    shares = []
    for ref, full, sent in ((w_ref, wp, wz), (m_ref, mp, mz)):
        rows = [ref[j] for j in range(3)]
        for j in range(3):
            full[j, own, :] = rows[j]
        sent[...] = jnp.concatenate(rows + [pad], axis=0).astype(BF16)

    pl.semaphore_wait(barrier, 8)
    cw = start(wz, wzr, ZW, zpeer)
    cm = start(mz, mzr, ZM, zpeer)
    hdoc = start(doc_ref, doch, HDOC, nxt)
    order = [(b, kv) for b in reversed(range(NBLK)) for kv in (0, 1)]
    halo = {b: [] for b in range(NBLK)}

    def send_halo(first, last):
        for b, kv in order[first:last]:
            rows = pl.ds(b * BLK, BLK)
            src, dst, num = ((k_ref, kh, HK), (v_ref, vh, HV))[kv]
            halo[b].append(start(src.at[rows], dst.at[rows], num + b, nxt))

    def gather_first(buf, base):
        return [
            start(buf.at[0, :, y, x], buf.at[0, :, y, x], base + d, xpeer[d]) for d in (1, 0, 2)
        ] + [
            start(buf.at[1, :, y, x], buf.at[1, :, y, x], base + 3 + d, ypeer[d]) for d in (1, 0, 2)
        ]

    def gather_second(buf, base, first):
        for copy in first[:3]:
            copy.wait_recv()
        copies = [
            start(buf.at[0, :, y], buf.at[0, :, y], base + 6 + d, ypeer[d]) for d in (1, 0, 2)
        ]
        for copy in first[3:]:
            copy.wait_recv()
        copies += [
            start(buf.at[1, :, :, x], buf.at[1, :, :, x], base + 9 + d, xpeer[d])
            for d in (1, 0, 2)
        ]
        return copies

    def set_pair(buf, value):
        value = value.astype(BF16)
        buf[0, :, y, x] = value[:, :, :128]
        buf[1, :, y, x] = value[:, :, 128:]

    def matrix(buf, j):
        return jnp.concatenate(
            [buf[0, j].reshape(HID, 128), buf[1, j].reshape(HID, 128)], axis=-1
        )

    kt[...] = k_ref[...].T
    pred = (-(rate_ref[...] / TOKENS) * v_ref[...].T.astype(F32)).astype(BF16)
    dpt[...] = pred
    dp[...] = pred.T
    dcol[...] = jnp.broadcast_to(doc_ref[...].astype(F32), (128, TOK)).T

    window = win_ref[0]

    def attend_own(b):
        n = (b + 1) * BLK
        rows = pl.ds(b * BLK, BLK)
        scores = dot_nn(q_ref[rows, :], kt[:, :n])
        qpos = b * BLK + lax.broadcasted_iota(jnp.int32, (BLK, 1), 0)
        kpos = lax.broadcasted_iota(jnp.int32, (1, n), 1)
        allowed = (kpos <= qpos) & (kpos > qpos - window)
        allowed = allowed & (doc_ref[:, :n].astype(F32) == dcol[rows, 0:1])
        scores = jnp.where(allowed, scores, NEG)
        top = jnp.max(scores, axis=-1, keepdims=True)
        expo = jnp.exp2((scores - top) * SCALE)
        m_s[rows, :] = top
        l_s[rows, :] = jnp.sum(expo, axis=-1, keepdims=True)
        acc[rows, :] = dot_nn(expo.astype(BF16), v_ref[:n, :])

    def attend_halo(b):
        for copy in halo[b]:
            copy.wait_recv()
        krows = pl.ds(b * BLK, BLK)
        keys, values = kh[krows, :], vh[krows, :]
        kdoc = doch[:, b * BLK : (b + 1) * BLK].astype(F32)
        reach = jnp.where(c == 0, -4 * TOK, window)

        def body(i, carry):
            rows = pl.ds(pl.multiple_of(i * BLK, BLK), BLK)
            scores = dot_nt(q_ref[rows, :], keys)
            qpos = i * BLK + lax.broadcasted_iota(jnp.int32, (BLK, 1), 0)
            kpos = b * BLK - TOK + lax.broadcasted_iota(jnp.int32, (1, BLK), 1)
            allowed = (kpos > qpos - reach) & (kdoc == dcol[rows, 0:1])
            scores = jnp.where(allowed, scores, NEG)
            old = m_s[rows, :]
            top = jnp.maximum(old, jnp.max(scores, axis=-1, keepdims=True))
            expo = jnp.exp2((scores - top) * SCALE)
            alpha = jnp.exp2((old - top) * SCALE)
            m_s[rows, :] = top
            l_s[rows, :] = l_s[rows, :] * alpha + jnp.sum(expo, axis=-1, keepdims=True)
            acc[rows, :] = acc[rows, :] * alpha + dot_nn(expo.astype(BF16), values)
            return carry

        lax.fori_loop(0, b + 1, body, 0)

    attend_own(0)
    attend_own(1)
    cw.wait_recv()
    got = wzr[...].astype(F32)
    for j in range(3):
        wp[j, far, :] = got[j * SHARE : (j + 1) * SHARE]
    set_pair(wall, wp[...])
    first = gather_first(wall, AG1)
    send_halo(*SENDS[0])
    attend_own(2)
    second = gather_second(wall, AG1, first)
    attend_own(3)
    cm.wait_recv()
    got = mzr[...].astype(F32)
    for j in range(3):
        mp[j, far, :] = got[j * SHARE : (j + 1) * SHARE]
    for copy in second:
        copy.wait_recv()

    def update(d, carry):
        yy = (y + 1 + d) % 4

        def part(j):
            return jnp.concatenate(
                [wall[0, j, yy].reshape(192, 128), wall[1, j, yy].reshape(192, 128)], axis=-1
            )

        gate = dot_nn(part(0), kt[...])
        up = dot_nn(part(1), kt[...])
        back = dot_nn(part(2), dpt[...])
        sig = 0.5 * jnp.tanh(0.5 * gate) + 0.5
        active = gate * sig
        hidden = (active * up).astype(BF16)
        d_gate = (back * up * (sig + active * (1.0 - sig))).astype(BF16)
        d_up = (back * active).astype(BF16)
        for j, g in enumerate(
            (dot_nn(d_gate, k_ref[...]), dot_nn(d_up, k_ref[...]), dot_nn(hidden, dp[...]))
        ):
            g = g.astype(BF16).reshape(4, PAIR, DH)
            grad[0, j, yy] = g[:, :, :128]
            grad[1, j, yy] = g[:, :, 128:]

        @pl.when(d < 3)
        def _():
            rcopy(grad.at[0, :, yy], rs1.at[0, d], RS + d, yy * 8 + x * 2 + zh).start()

        for e in range(3):
            rcopy(
                grad.at[1, :, yy, (x + e + 1) % 4], rs1.at[1, e, :, yy], RS + 3 + e, xpeer[e]
            ).start()
        return carry

    lax.fori_loop(0, 4, update, 0)

    r1a = [
        rcopy(grad.at[0, :, (y + d + 1) % 4], rs1.at[0, d], RS + d, ypeer[d]) for d in range(3)
    ]
    r1b = [
        rcopy(grad.at[1, :, :, (x + d + 1) % 4], rs1.at[1, d], RS + 3 + d, xpeer[d])
        for d in range(3)
    ]
    started.extend(r1a + r1b)
    send_halo(*SENDS[1])
    for copy in r1a:
        copy.wait_recv()
    rs2s[0] = sum([rs1[0, d].astype(F32) for d in range(3)], grad[0, :, y].astype(F32)).astype(
        BF16
    )
    r2a = [
        start(rs2s.at[0, :, (x + d + 1) % 4], rs2.at[0, d], RS + 6 + d, xpeer[d]) for d in range(3)
    ]
    for copy in r1b:
        copy.wait_recv()
    rs2s[1] = sum(
        [rs1[1, d].astype(F32) for d in range(3)], grad[1, :, :, x].astype(F32)
    ).astype(BF16)
    r2b = [
        start(rs2s.at[1, :, (y + d + 1) % 4], rs2.at[1, d], RS + 9 + d, ypeer[d]) for d in range(3)
    ]
    cz = []
    for half, copies, mine in ((0, r2a, x), (1, r2b, y)):
        lanes = slice(half * 128, half * 128 + 128)
        for copy in copies:
            copy.wait_recv()
        value = sum([rs2[half, d].astype(F32) for d in range(3)], rs2s[half, :, mine].astype(F32))
        tot[:, :, lanes] = value
        totb[half] = value.astype(BF16)
        cz.append(start(totb.at[half], totz.at[half], ZG + half, zpeer))
    send_halo(*SENDS[2])
    hdoc.wait_recv()
    attend_halo(3)
    for copy in cz:
        copy.wait_recv()
    tot[...] += jnp.concatenate([totz[0], totz[1]], axis=-1).astype(F32)

    weights = wp[...]
    moment = 0.9 * mp[...] + tot[...]
    stepped = weights - moment
    factor = jnp.sqrt(jnp.mean(weights * weights, axis=-1, keepdims=True)) / jnp.sqrt(
        jnp.mean(stepped * stepped, axis=-1, keepdims=True) + 1e-06
    )
    fresh = stepped * factor
    set_pair(wnew, fresh)
    first = gather_first(wnew, AG2)
    nwp[...] = fresh
    nmp[...] = moment
    for j in range(3):
        nw_ref[j] = nwp[j, own, :]
        nm_ref[j] = nmp[j, own, :]
    second = gather_second(wnew, AG2, first)
    attend_halo(2)
    for copy in second:
        copy.wait_recv()

    new_gate, new_up, new_down = matrix(wnew, 0), matrix(wnew, 1), matrix(wnew, 2)
    gain = gain_ref[...]
    for b in range(NBLK):
        rows = pl.ds(b * BLK, BLK)
        gate = dot_nt(q_ref[rows, :], new_gate)
        up = dot_nt(q_ref[rows, :], new_up)
        sig = 0.5 * jnp.tanh(0.5 * gate) + 0.5
        fast = dot_nn((gate * sig * up).astype(BF16), new_down)
        mean = jnp.mean(fast * fast, axis=-1, keepdims=True)
        normed[rows, :] = fast * lax.rsqrt(mean + 1e-06) * gain

    for b in (1, 0):
        attend_halo(b)
    for b in range(NBLK):
        rows = pl.ds(b * BLK, BLK)
        out_ref[rows, :] = (acc[rows, :] / l_s[rows, :] + normed[rows, :]).astype(BF16)
    for copy in started:
        copy.wait_send()


def local(queries, keys, values, rates, doc_ids, windows, fast_weights, momentum, out_gain):
    vmem = pl.BlockSpec(memory_space=pltpu.VMEM)
    smem = pl.BlockSpec(memory_space=pltpu.SMEM)
    plane = (2, 3, 4, 4, PAIR, 128)
    mixed, new_w, new_m = pl.pallas_call(
        kernel,
        out_shape=(
            pltpu.VMEM((TOK, DH), BF16),
            pltpu.VMEM((3, SHARE, DH), F32),
            pltpu.VMEM((3, SHARE, DH), F32),
        ),
        in_specs=[smem] + [vmem] * 8,
        out_specs=(vmem, vmem, vmem),
        scratch_shapes=[
            pltpu.VMEM((DH, TOK), BF16),
            pltpu.VMEM((TOK, DH), BF16),
            pltpu.VMEM((DH, TOK), BF16),
            pltpu.VMEM((TOK, DH), BF16),
            pltpu.VMEM((TOK, DH), BF16),
            pltpu.VMEM((1, TOK), jnp.int32),
            pltpu.VMEM((TOK, 128), F32),
            pltpu.VMEM((80, DH), BF16),
            pltpu.VMEM((80, DH), BF16),
            pltpu.VMEM((80, DH), BF16),
            pltpu.VMEM((80, DH), BF16),
            pltpu.VMEM((3, PAIR, DH), F32),
            pltpu.VMEM((3, PAIR, DH), F32),
            pltpu.VMEM(plane, BF16),
            pltpu.VMEM(plane, BF16),
            pltpu.VMEM(plane, BF16),
            pltpu.VMEM((2, 3, 3, 4, PAIR, 128), BF16),
            pltpu.VMEM((2, 3, 4, PAIR, 128), BF16),
            pltpu.VMEM((2, 3, 3, PAIR, 128), BF16),
            pltpu.VMEM((3, PAIR, DH), F32),
            pltpu.VMEM((2, 3, PAIR, 128), BF16),
            pltpu.VMEM((2, 3, PAIR, 128), BF16),
            pltpu.VMEM((3, PAIR, DH), F32),
            pltpu.VMEM((3, PAIR, DH), F32),
            pltpu.VMEM((TOK, DH), F32),
            pltpu.VMEM((TOK, 1), F32),
            pltpu.VMEM((TOK, 1), F32),
            pltpu.VMEM((TOK, DH), F32),
            pltpu.SemaphoreType.DMA((NSEM,)),
            pltpu.SemaphoreType.DMA((NSEM,)),
        ],
        compiler_params=pltpu.CompilerParams(
            collective_id=0, has_side_effects=True, vmem_limit_bytes=56 * 2**20
        ),
        name="ttt_layer",
    )(
        windows,
        queries,
        keys,
        values,
        rates.reshape(1, TOK),
        doc_ids.reshape(1, TOK),
        fast_weights.reshape(3, DH, SHARE).transpose(0, 2, 1),
        momentum.reshape(3, DH, SHARE).transpose(0, 2, 1),
        out_gain,
    )
    new_w, new_m = (
        part.transpose(0, 2, 1).reshape(3, 1, DH, SHARE) for part in (new_w, new_m)
    )
    return mixed, new_w, new_m


def solution(mesh):
    in_specs = (
        P("ctx", "head"),
        P("ctx", "head"),
        P("ctx", "head"),
        P("ctx", "head"),
        P("ctx"),
        P("head"),
        P(None, "head", None, "ctx"),
        P(None, "head", None, "ctx"),
        P("head", None),
    )
    out_specs = (P("ctx", "head"), P(None, "head", None, "ctx"), P(None, "head", None, "ctx"))
    return jax.shard_map(local, mesh=mesh, in_specs=in_specs, out_specs=out_specs, check_vma=False)
```

```python
import functools
import math

import jax
import jax.numpy as jnp
from jax import lax
from jax.experimental import pallas as pl
from jax.experimental.pallas import tpu as pltpu
from jax.sharding import PartitionSpec as P

DH = 256
HID = 768
TOK = 1024
SHARE = 24
PAIR = 48
TOKENS = 32768
BLK = 256
NBLK = TOK // BLK
MESH = pl.DeviceIdType.MESH
SCALE = math.log2(math.e) / 16.0
NEG = -1e30
SENDS = ((0, 6), (6, 6), (6, 8))
F32 = jnp.float32
BF16 = jnp.bfloat16

ZW, ZM, HDOC, ZG = 0, 1, 2, 3
HK, HV = 5, 9
AG1, RS, AG2 = 13, 25, 37
NSEM = 49


def dot_nn(a, b):
    return jnp.dot(a, b, preferred_element_type=F32)


def dot_nt(a, b):
    return lax.dot_general(a, b, (((1,), (1,)), ((), ())), preferred_element_type=F32)


def kernel(
    win_ref, q_ref, k_ref, v_ref, rate_ref, doc_ref, w_ref, m_ref, gain_ref,
    out_ref, nw_ref, nm_ref,
    kt, dp, dpt, kh, vh, doch, dcol,
    wz, mz, wzr, mzr, wp, mp,
    wall, wnew, grad, rs1, rs2s, rs2, tot, totb, totz, nwp, nmp,
    acc, m_s, l_s, normed,
    ssem, rsem,
):
    c, h = lax.axis_index("ctx"), lax.axis_index("head")
    y, x, zh = c // 8, (c // 2) % 4, c % 2
    zpeer = c + 1 - 2 * zh
    nxt, prv = (c + 1) % 32, (c + 31) % 32
    other = (c + 31 + 2 * zh) % 32
    xpeer = [y * 8 + ((x + d) % 4) * 2 + zh for d in (1, 2, 3)]
    ypeer = [((y + d) % 4) * 8 + x * 2 + zh for d in (1, 2, 3)]

    barrier = pltpu.get_barrier_semaphore()
    for peer in [zpeer, other] + xpeer + ypeer:
        pl.semaphore_signal(barrier, inc=1, device_id=(peer, h), device_id_type=MESH)

    def rcopy(src, dst, num, ctx):
        return pltpu.make_async_remote_copy(
            src_ref=src, dst_ref=dst, send_sem=ssem.at[num], recv_sem=rsem.at[num],
            device_id=(ctx, h), device_id_type=MESH,
        )

    started = []

    def start(src, dst, num, ctx):
        copy = rcopy(src, dst, num, ctx)
        copy.start()
        started.append(copy)
        return copy

    own = pl.ds(pl.multiple_of(zh * SHARE, 8), SHARE)
    far = pl.ds(pl.multiple_of((1 - zh) * SHARE, 8), SHARE)
    pad = jnp.zeros((8, DH), F32)
    shares = []
    for ref, full, sent in ((w_ref, wp, wz), (m_ref, mp, mz)):
        rows = [ref[j] for j in range(3)]
        for j in range(3):
            full[j, own, :] = rows[j]
        sent[...] = jnp.concatenate(rows + [pad], axis=0).astype(BF16)

    pl.semaphore_wait(barrier, 8)
    cw = start(wz, wzr, ZW, zpeer)
    cm = start(mz, mzr, ZM, zpeer)
    hdoc = start(doc_ref, doch, HDOC, nxt)
    order = [(b, kv) for b in reversed(range(NBLK)) for kv in (0, 1)]
    halo = {b: [] for b in range(NBLK)}

    def send_halo(first, last):
        for b, kv in order[first:last]:
            rows = pl.ds(b * BLK, BLK)
            src, dst, num = ((k_ref, kh, HK), (v_ref, vh, HV))[kv]
            halo[b].append(start(src.at[rows], dst.at[rows], num + b, nxt))

    def gather_first(buf, base):
        return [
            start(buf.at[0, :, y, x], buf.at[0, :, y, x], base + d, xpeer[d]) for d in (1, 0, 2)
        ] + [
            start(buf.at[1, :, y, x], buf.at[1, :, y, x], base + 3 + d, ypeer[d]) for d in (1, 0, 2)
        ]

    def gather_second(buf, base, first):
        for copy in first[:3]:
            copy.wait_recv()
        copies = [
            start(buf.at[0, :, y], buf.at[0, :, y], base + 6 + d, ypeer[d]) for d in (1, 0, 2)
        ]
        for copy in first[3:]:
            copy.wait_recv()
        copies += [
            start(buf.at[1, :, :, x], buf.at[1, :, :, x], base + 9 + d, xpeer[d])
            for d in (1, 0, 2)
        ]
        return copies

    def set_pair(buf, value):
        value = value.astype(BF16)
        buf[0, :, y, x] = value[:, :, :128]
        buf[1, :, y, x] = value[:, :, 128:]

    def matrix(buf, j):
        return jnp.concatenate(
            [buf[0, j].reshape(HID, 128), buf[1, j].reshape(HID, 128)], axis=-1
        )

    kt[...] = k_ref[...].T
    pred = (-(rate_ref[...] / TOKENS) * v_ref[...].T.astype(F32)).astype(BF16)
    dpt[...] = pred
    dp[...] = pred.T
    dcol[...] = jnp.broadcast_to(doc_ref[...].astype(F32), (128, TOK)).T

    window = win_ref[0]

    def attend_own(b):
        n = (b + 1) * BLK
        rows = pl.ds(b * BLK, BLK)
        scores = dot_nn(q_ref[rows, :], kt[:, :n])
        qpos = b * BLK + lax.broadcasted_iota(jnp.int32, (BLK, 1), 0)
        kpos = lax.broadcasted_iota(jnp.int32, (1, n), 1)
        allowed = (kpos <= qpos) & (kpos > qpos - window)
        allowed = allowed & (doc_ref[:, :n].astype(F32) == dcol[rows, 0:1])
        scores = jnp.where(allowed, scores, NEG)
        top = jnp.max(scores, axis=-1, keepdims=True)
        expo = jnp.exp2((scores - top) * SCALE)
        m_s[rows, :] = top
        l_s[rows, :] = jnp.sum(expo, axis=-1, keepdims=True)
        acc[rows, :] = dot_nn(expo.astype(BF16), v_ref[:n, :])

    def attend_halo(b):
        for copy in halo[b]:
            copy.wait_recv()
        krows = pl.ds(b * BLK, BLK)
        keys, values = kh[krows, :], vh[krows, :]
        kdoc = doch[:, b * BLK : (b + 1) * BLK].astype(F32)
        reach = jnp.where(c == 0, -4 * TOK, window)

        def body(i, carry):
            rows = pl.ds(pl.multiple_of(i * BLK, BLK), BLK)
            scores = dot_nt(q_ref[rows, :], keys)
            qpos = i * BLK + lax.broadcasted_iota(jnp.int32, (BLK, 1), 0)
            kpos = b * BLK - TOK + lax.broadcasted_iota(jnp.int32, (1, BLK), 1)
            allowed = (kpos > qpos - reach) & (kdoc == dcol[rows, 0:1])
            scores = jnp.where(allowed, scores, NEG)
            old = m_s[rows, :]
            top = jnp.maximum(old, jnp.max(scores, axis=-1, keepdims=True))
            expo = jnp.exp2((scores - top) * SCALE)
            alpha = jnp.exp2((old - top) * SCALE)
            m_s[rows, :] = top
            l_s[rows, :] = l_s[rows, :] * alpha + jnp.sum(expo, axis=-1, keepdims=True)
            acc[rows, :] = acc[rows, :] * alpha + dot_nn(expo.astype(BF16), values)
            return carry

        lax.fori_loop(0, b + 1, body, 0)

    attend_own(0)
    attend_own(1)
    cw.wait_recv()
    got = wzr[...].astype(F32)
    for j in range(3):
        wp[j, far, :] = got[j * SHARE : (j + 1) * SHARE]
    set_pair(wall, wp[...])
    first = gather_first(wall, AG1)
    send_halo(*SENDS[0])
    attend_own(2)
    second = gather_second(wall, AG1, first)
    attend_own(3)
    cm.wait_recv()
    got = mzr[...].astype(F32)
    for j in range(3):
        mp[j, far, :] = got[j * SHARE : (j + 1) * SHARE]
    for copy in second:
        copy.wait_recv()

    def update(d, carry):
        yy = (y + 1 + d) % 4

        def part(j):
            return jnp.concatenate(
                [wall[0, j, yy].reshape(192, 128), wall[1, j, yy].reshape(192, 128)], axis=-1
            )

        gate = dot_nn(part(0), kt[...])
        up = dot_nn(part(1), kt[...])
        back = dot_nn(part(2), dpt[...])
        sig = 0.5 * jnp.tanh(0.5 * gate) + 0.5
        active = gate * sig
        hidden = (active * up).astype(BF16)
        d_gate = (back * up * (sig + active * (1.0 - sig))).astype(BF16)
        d_up = (back * active).astype(BF16)
        for j, g in enumerate(
            (dot_nn(d_gate, k_ref[...]), dot_nn(d_up, k_ref[...]), dot_nn(hidden, dp[...]))
        ):
            g = g.astype(BF16).reshape(4, PAIR, DH)
            grad[0, j, yy] = g[:, :, :128]
            grad[1, j, yy] = g[:, :, 128:]

        @pl.when(d < 3)
        def _():
            rcopy(grad.at[0, :, yy], rs1.at[0, d], RS + d, yy * 8 + x * 2 + zh).start()

        for e in range(3):
            rcopy(
                grad.at[1, :, yy, (x + e + 1) % 4], rs1.at[1, e, :, yy], RS + 3 + e, xpeer[e]
            ).start()
        return carry

    lax.fori_loop(0, 4, update, 0)

    r1a = [
        rcopy(grad.at[0, :, (y + d + 1) % 4], rs1.at[0, d], RS + d, ypeer[d]) for d in range(3)
    ]
    r1b = [
        rcopy(grad.at[1, :, :, (x + d + 1) % 4], rs1.at[1, d], RS + 3 + d, xpeer[d])
        for d in range(3)
    ]
    started.extend(r1a + r1b)
    send_halo(*SENDS[1])
    for copy in r1a:
        copy.wait_recv()
    rs2s[0] = sum([rs1[0, d].astype(F32) for d in range(3)], grad[0, :, y].astype(F32)).astype(
        BF16
    )
    r2a = [
        start(rs2s.at[0, :, (x + d + 1) % 4], rs2.at[0, d], RS + 6 + d, xpeer[d]) for d in range(3)
    ]
    for copy in r1b:
        copy.wait_recv()
    rs2s[1] = sum(
        [rs1[1, d].astype(F32) for d in range(3)], grad[1, :, :, x].astype(F32)
    ).astype(BF16)
    r2b = [
        start(rs2s.at[1, :, (y + d + 1) % 4], rs2.at[1, d], RS + 9 + d, ypeer[d]) for d in range(3)
    ]
    cz = []
    for half, copies, mine in ((0, r2a, x), (1, r2b, y)):
        lanes = slice(half * 128, half * 128 + 128)
        for copy in copies:
            copy.wait_recv()
        value = sum([rs2[half, d].astype(F32) for d in range(3)], rs2s[half, :, mine].astype(F32))
        tot[:, :, lanes] = value
        totb[half] = value.astype(BF16)
        cz.append(start(totb.at[half], totz.at[half], ZG + half, zpeer))
    send_halo(*SENDS[2])
    hdoc.wait_recv()
    attend_halo(3)
    for copy in cz:
        copy.wait_recv()
    tot[...] += jnp.concatenate([totz[0], totz[1]], axis=-1).astype(F32)

    weights = wp[...]
    moment = 0.9 * mp[...] + tot[...]
    stepped = weights - moment
    factor = jnp.sqrt(jnp.mean(weights * weights, axis=-1, keepdims=True)) / jnp.sqrt(
        jnp.mean(stepped * stepped, axis=-1, keepdims=True) + 1e-06
    )
    fresh = stepped * factor
    set_pair(wnew, fresh)
    first = gather_first(wnew, AG2)
    nwp[...] = fresh
    nmp[...] = moment
    for j in range(3):
        nw_ref[j] = nwp[j, own, :]
        nm_ref[j] = nmp[j, own, :]
    second = gather_second(wnew, AG2, first)
    attend_halo(2)
    for copy in second:
        copy.wait_recv()

    new_gate, new_up, new_down = matrix(wnew, 0), matrix(wnew, 1), matrix(wnew, 2)
    gain = gain_ref[...]
    for b in range(NBLK):
        rows = pl.ds(b * BLK, BLK)
        gate = dot_nt(q_ref[rows, :], new_gate)
        up = dot_nt(q_ref[rows, :], new_up)
        sig = 0.5 * jnp.tanh(0.5 * gate) + 0.5
        fast = dot_nn((gate * sig * up).astype(BF16), new_down)
        mean = jnp.mean(fast * fast, axis=-1, keepdims=True)
        normed[rows, :] = fast * lax.rsqrt(mean + 1e-06) * gain

    def finish(b):
        rows = pl.ds(b * BLK, BLK)
        out_ref[rows, :] = (acc[rows, :] / l_s[rows, :] + normed[rows, :]).astype(BF16)

    finish(3)
    finish(2)
    for b in (1, 0):
        attend_halo(b)
        finish(b)
    for copy in started:
        copy.wait_send()


def local(queries, keys, values, rates, doc_ids, windows, fast_weights, momentum, out_gain):
    vmem = pl.BlockSpec(memory_space=pltpu.VMEM)
    smem = pl.BlockSpec(memory_space=pltpu.SMEM)
    plane = (2, 3, 4, 4, PAIR, 128)
    mixed, new_w, new_m = pl.pallas_call(
        kernel,
        out_shape=(
            pltpu.VMEM((TOK, DH), BF16),
            pltpu.VMEM((3, SHARE, DH), F32),
            pltpu.VMEM((3, SHARE, DH), F32),
        ),
        in_specs=[smem] + [vmem] * 8,
        out_specs=(vmem, vmem, vmem),
        scratch_shapes=[
            pltpu.VMEM((DH, TOK), BF16),
            pltpu.VMEM((TOK, DH), BF16),
            pltpu.VMEM((DH, TOK), BF16),
            pltpu.VMEM((TOK, DH), BF16),
            pltpu.VMEM((TOK, DH), BF16),
            pltpu.VMEM((1, TOK), jnp.int32),
            pltpu.VMEM((TOK, 128), F32),
            pltpu.VMEM((80, DH), BF16),
            pltpu.VMEM((80, DH), BF16),
            pltpu.VMEM((80, DH), BF16),
            pltpu.VMEM((80, DH), BF16),
            pltpu.VMEM((3, PAIR, DH), F32),
            pltpu.VMEM((3, PAIR, DH), F32),
            pltpu.VMEM(plane, BF16),
            pltpu.VMEM(plane, BF16),
            pltpu.VMEM(plane, BF16),
            pltpu.VMEM((2, 3, 3, 4, PAIR, 128), BF16),
            pltpu.VMEM((2, 3, 4, PAIR, 128), BF16),
            pltpu.VMEM((2, 3, 3, PAIR, 128), BF16),
            pltpu.VMEM((3, PAIR, DH), F32),
            pltpu.VMEM((2, 3, PAIR, 128), BF16),
            pltpu.VMEM((2, 3, PAIR, 128), BF16),
            pltpu.VMEM((3, PAIR, DH), F32),
            pltpu.VMEM((3, PAIR, DH), F32),
            pltpu.VMEM((TOK, DH), F32),
            pltpu.VMEM((TOK, 1), F32),
            pltpu.VMEM((TOK, 1), F32),
            pltpu.VMEM((TOK, DH), F32),
            pltpu.SemaphoreType.DMA((NSEM,)),
            pltpu.SemaphoreType.DMA((NSEM,)),
        ],
        compiler_params=pltpu.CompilerParams(
            collective_id=0, has_side_effects=True, vmem_limit_bytes=56 * 2**20
        ),
        name="ttt_layer",
    )(
        windows,
        queries,
        keys,
        values,
        rates.reshape(1, TOK),
        doc_ids.reshape(1, TOK),
        fast_weights.reshape(3, DH, SHARE).transpose(0, 2, 1),
        momentum.reshape(3, DH, SHARE).transpose(0, 2, 1),
        out_gain,
    )
    new_w, new_m = (
        part.transpose(0, 2, 1).reshape(3, 1, DH, SHARE) for part in (new_w, new_m)
    )
    return mixed, new_w, new_m


def solution(mesh):
    in_specs = (
        P("ctx", "head"),
        P("ctx", "head"),
        P("ctx", "head"),
        P("ctx", "head"),
        P("ctx"),
        P("head"),
        P(None, "head", None, "ctx"),
        P(None, "head", None, "ctx"),
        P("head", None),
    )
    out_specs = (P("ctx", "head"), P(None, "head", None, "ctx"), P(None, "head", None, "ctx"))
    return jax.shard_map(local, mesh=mesh, in_specs=in_specs, out_specs=out_specs, check_vma=False)
```
